512 devices in a mesh: row: 32 (over z, core), col: 16 (over x, y).
Axes of the slice: x: 4, y: 4, z: 16, core: 2. Of those that a mesh axis runs over, the one named last changes fastest.
Arguments:
- factor: bfloat16 [128, 16, 8, 128, 128], P('row', 'col'), may hold values from -0.0625 to 0.0625
- index: int32 [128, 16, 8], P('row', 'col'), may hold values from 0 to 15, as said below
- keep: int32 [128, 16, 8, 16], P('row', 'col'), may hold values 0 or 1
- panel: bfloat16 [256, 16, 128, 128], P('col', None, 'row'), may hold values from -6 to 6
Outputs:
- mixed: bfloat16 [128, 16, 128, 128], P('row', 'col')
The draws below stay inside these ranges and needn't reach their ends.
Inputs may be any that keep to these rules, and one draw needn't show every extreme that they name: For each block row and each index of col, the 8 entries are distinct.
All inputs are finite; a program needn't handle non-finite values. No bound on the sum of `keep` on one device may be relied on, other than what follows from the above.
Results may differ from the reference program's by a relative error of at most 0.001.
Values may be sent and summed in bfloat16 or wider, within the bound.
No kernel may reach another device: no remote copies, remote signals or barrier semaphores. Data moves between devices by JAX's collectives and lax.ppermute only.
A program may use at most 64 MiB of HBM per device.

```python
import jax
import jax.numpy as jnp
from jax import lax

B = 128
NBC = 16
KFC = 8
NB = 128
NK = 256
KF = 128
N_COL = 16


def draw_index(key, part):
    key = jax.random.fold_in(key, 11)
    scores = jax.random.randint(key, (NB, N_COL, NBC), 0, 1048576, dtype=jnp.int32)
    scores = scores * NBC + jnp.arange(NBC, dtype=jnp.int32)
    order = jnp.argsort(scores, axis=-1)
    return order[:, :, :KFC].astype(jnp.int32)


def place_ends(values, own_key, least, largest):
    spot = [jax.random.randint(jax.random.fold_in(own_key, axis), (), 0, length) for axis, length in enumerate(values.shape)]
    widest = values.shape.index(max(values.shape))
    next_to = spot[:widest] + [(spot[widest] + 1) % values.shape[widest]] + spot[widest + 1:]
    return values.at[tuple(spot)].set(least).at[tuple(next_to)].set(largest)


def block_scale(own_key, shape, shards, smallest, top_value):
    def one(axis_at, shards_of):
        steps = jax.random.uniform(jax.random.fold_in(jax.random.fold_in(own_key, 6), axis_at), (shards_of,), jnp.float32, smallest / len(shards), top_value / len(shards))
        return jnp.repeat(jnp.exp(steps), shape[axis_at] // shards_of).reshape((-1,) + (1,) * (len(shape) - axis_at - 1))

    loudness = one(*shards[0])
    for cut in shards[1:]:
        loudness = loudness * one(*cut)
    return loudness


def centred(key, shape, spread, limit, split=(), kind=jnp.bfloat16):
    array = jax.random.normal(key, shape, jnp.float32) * spread
    if len(split) > 0:
        array = block_scale(key, shape, split, -0.22, 0.18) * array
    return jnp.clip(array, min=-limit, max=limit).astype(kind)


def setup_inputs(seed: int = 0) -> dict:
    key_of = jax.random.split(jax.random.key(seed), 5)
    return {
        "factor": centred(key_of[0], (NB, N_COL, KFC, B, B), (B * KFC * N_COL // 2) ** -0.5, 0.0625, ((0, 32), (1, 16))),
        "index": draw_index(jax.random.fold_in(key_of[4], 71), 0),
        "keep": place_ends((jax.random.randint(key_of[2], (NB, N_COL, KFC, N_COL), 0, 2) < 1).astype(jnp.int32), jax.random.fold_in(key_of[2], 1), 0, 1),
        "panel": centred(key_of[3], (NK, N_COL, B, B), 1.0, 6.0, ((0, 16), (2, 32))),
    }


def reference(factor, index, keep, panel):
    def row_product(inputs):
        factor_row, index_row, keep_row = inputs
        block_starts = jnp.arange(N_COL, dtype=jnp.int32)[:, None] * NBC
        index_all = (block_starts + index_row.astype(jnp.int32)).reshape(KF).astype(jnp.int32)
        chosen_blocks = panel[index_all].astype(jnp.float32)
        mask_all = keep_row.reshape(KF, N_COL).astype(jnp.float32)
        pattern_masked = chosen_blocks * mask_all[:, :, None, None]
        factor_flat = factor_row.reshape(KF, B, B).astype(jnp.float32)
        result = jnp.einsum('nab,ngbd->gad', factor_flat, pattern_masked)
        return result.astype(jnp.bfloat16)

    return lax.map(row_product, (factor, index, keep))
```

```python
import jax
import jax.numpy as jnp
from jax import lax
from jax.experimental import pallas as pl
from jax.experimental.pallas import tpu as pltpu
from jax.sharding import PartitionSpec as P

ROWS = 32
COLS = 16
NBC = 16
SUB = 4
B = 128
DEPTH = NBC * B


def spread_kernel(index_ref, factor_ref, spread_ref):
    i = pl.program_id(0)
    b = lax.broadcasted_iota(jnp.int32, (B, DEPTH), 0)
    col = lax.broadcasted_iota(jnp.int32, (B, DEPTH), 1)
    home = (col // (NBC * SUB)) * SUB + col % SUB
    place = jnp.where(b == home, 1.0, 0.0).astype(jnp.bfloat16)
    block = (lax.broadcasted_iota(jnp.int32, (1, DEPTH), 1) // SUB) % NBC
    total = jnp.zeros((B, DEPTH), jnp.float32)
    for s in range(factor_ref.shape[1]):
        moved = jnp.dot(factor_ref[0, s], place, preferred_element_type=jnp.float32)
        total = jnp.where(block == index_ref[i, s], moved, total)
    spread_ref[0] = total.astype(jnp.bfloat16)


def product_kernel(spread_ref, mask_ref, panel_ref, out_ref):
    rows = panel_ref[:, 0].reshape(DEPTH, B)
    for i in range(spread_ref.shape[0]):
        out_ref[0, i] = jnp.dot(
            spread_ref[i] * mask_ref[0, i : i + 1], rows, preferred_element_type=jnp.float32
        )


def per_device(factor, index, keep, panel):
    n_i = factor.shape[0]
    factor, index, keep = factor[:, 0], index[:, 0], keep[:, 0]
    shard = panel.transpose(1, 0, 2, 3).reshape(COLS, NBC * SUB, B)
    gathered = lax.all_gather(shard, "row", axis=0)

    spread = pl.pallas_call(
        spread_kernel,
        grid=(n_i,),
        in_specs=[
            pl.BlockSpec(memory_space=pltpu.SMEM),
            pl.BlockSpec((1,) + factor.shape[1:], lambda i: (i, 0, 0, 0)),
        ],
        out_specs=pl.BlockSpec((1, B, DEPTH), lambda i: (i, 0, 0)),
        out_shape=jax.ShapeDtypeStruct((n_i, B, DEPTH), jnp.bfloat16),
        compiler_params=pltpu.CompilerParams(vmem_limit_bytes=32 * 2**20),
        cost_estimate=pl.CostEstimate(flops=2 * n_i * 8 * B * B * DEPTH, bytes_accessed=3 * 2**20, transcendentals=0),
    )(index, factor)

    chosen = (index[:, :, None] == jnp.arange(NBC)).astype(jnp.float32)
    kept = jnp.einsum("isk,isg->gik", chosen, keep.astype(jnp.float32))
    mask = jnp.broadcast_to(
        kept.astype(jnp.bfloat16)[:, :, None, :, None], (COLS, n_i, ROWS, NBC, SUB)
    ).reshape(COLS, n_i, DEPTH)

    partial = pl.pallas_call(
        product_kernel,
        grid=(COLS,),
        in_specs=[
            pl.BlockSpec((n_i, B, DEPTH), lambda g: (0, 0, 0)),
            pl.BlockSpec((1, n_i, DEPTH), lambda g: (g, 0, 0)),
            pl.BlockSpec((ROWS, 1, NBC * SUB, B), lambda g: (0, g, 0, 0)),
        ],
        out_specs=pl.BlockSpec((1, n_i, B, B), lambda g: (g, 0, 0, 0)),
        out_shape=jax.ShapeDtypeStruct((COLS, n_i, B, B), jnp.float32),
        compiler_params=pltpu.CompilerParams(vmem_limit_bytes=58 * 2**20),
        cost_estimate=pl.CostEstimate(flops=2 * COLS * n_i * B * B * DEPTH, bytes_accessed=15 * 2**20, transcendentals=0),
    )(spread, mask, gathered)

    parts = lax.all_to_all(partial, "col", 0, 0, tiled=True)
    return jnp.sum(parts, axis=0).astype(jnp.bfloat16)[:, None]


def solution(mesh):
    return jax.shard_map(
        per_device,
        mesh=mesh,
        in_specs=(
            P("row", "col", None, None, None),
            P("row", "col", None),
            P("row", "col", None, None),
            P("col", None, "row", None),
        ),
        out_specs=P("row", "col", None, None),
        check_vma=False,
    )
```

```python
import jax
import jax.numpy as jnp
from jax import lax
from jax.experimental import pallas as pl
from jax.experimental.pallas import tpu as pltpu
from jax.sharding import Mesh, PartitionSpec as P

ROWS = 32
NX = 4
NY = 4
NBC = 16
KFC = 8
SUB = 4
B = 128
CHUNK = NBC * SUB
PER_X = NY * CHUNK
SHARD = NX * PER_X
EXTRA = 16
MIB = 2**20


def code_kernel(shard_ref, code_ref):
    top = jnp.float32(0.0)
    for x in range(NX):
        top = jnp.maximum(top, jnp.max(jnp.abs(shard_ref[x, :PER_X].astype(jnp.float32))))
    lane = lax.broadcasted_iota(jnp.int32, (8, 128), 1)
    power = jnp.int32(126)
    scale = jnp.float32(2.0**126)
    for e in range(-96, 3):
        above = top >= jnp.float32(2.0**e)
        power = jnp.where(above, jnp.int32(29 - e), power)
        scale = jnp.where(above, jnp.float32(2.0 ** (29 - e)), scale)
    for x in range(NX):

        def step(t, carry):
            rows = pl.ds(pl.multiple_of(t * 16, 16), 16)
            value = shard_ref[x, rows].astype(jnp.float32) * scale
            size = jnp.abs(value)
            shift = jnp.zeros(value.shape, jnp.int32)
            down = jnp.ones(value.shape, jnp.float32)
            for s in range(1, 23):
                above = size >= jnp.float32(2.0 ** (7 + s))
                shift = jnp.where(above, jnp.int32(s * 512 + 256), shift)
                down = jnp.where(above, jnp.float32(2.0**-s), down)
            shift = jnp.where(shift == 0, 256, shift)
            mantissa = jnp.round(value * down).astype(jnp.int32)
            code_ref[pl.ds(pl.multiple_of(x * PER_X + t * 16, 16), 16)] = (shift + mantissa).astype(jnp.int16)
            return carry

        lax.fori_loop(0, PER_X // 16, step, 0)
    code_ref[SHARD:] = jnp.full((EXTRA, B), power, jnp.int32).astype(jnp.int16)


def product_kernel(y_ref, index_ref, keep_ref, factor_ref, panel_ref, *refs):
    out_refs, (block_ref, total_ref, scale_ref) = refs[:NY], refs[NY:]
    x = pl.program_id(0)
    y = y_ref[0]

    @pl.when(x == 0)
    def _():
        power = panel_ref[:, SHARD : SHARD + EXTRA].astype(jnp.int32)
        scale = jnp.ones(power.shape, jnp.float32)
        for bit in range(7):
            on = (power & (1 << bit)) > 0
            scale = scale * jnp.where(on, jnp.float32(2.0 ** -(1 << bit)), jnp.float32(1.0))
        scale_ref[...] = scale[:, :8]

    low = lax.broadcasted_iota(jnp.int32, (NBC // 2, 8, B), 1) < SUB

    def spread(q, carry):
        scales = [scale_ref[q * 4 + r] for r in range(4)]
        for t in range(NY):
            g = lax.rem(y + t, NY)
            rows = pl.ds(pl.multiple_of(x * PER_X + g * CHUNK, CHUNK), CHUNK)
            piece = []
            for r in range(4):
                code = panel_ref[q * 4 + r, rows].astype(jnp.int32)
                value = lax.shift_left((code & 511) - 256, lax.shift_right_logical(code, 9))
                piece.append(value.astype(jnp.float32).reshape(NBC // 2, 8, B) * scales[r])
            even, odd = [], []
            for a, b in ((piece[0], piece[1]), (piece[2], piece[3])):
                even.append(jnp.where(low, a, pltpu.roll(b, SUB, 1)))
                odd.append(jnp.where(low, pltpu.roll(a, SUB, 1), b))
            at = pl.ds(pl.multiple_of(q * 16, 16), 16)
            lanes = slice(t * B, (t + 1) * B)
            block_ref[:, 0, at, lanes] = jnp.concatenate(even, axis=1).astype(jnp.bfloat16)
            block_ref[:, 1, at, lanes] = jnp.concatenate(odd, axis=1).astype(jnp.bfloat16)
        return carry

    lax.fori_loop(0, ROWS // 4, spread, 0)

    n_i = total_ref.shape[0]

    def multiply(i, carry):
        total = jnp.zeros((B, NY * B), jnp.float32)
        for s in range(0, KFC, 2):
            left, right = [], []
            for u in (s, s + 1):
                left.append(factor_ref[0, i, u])
                k = index_ref[(x * n_i + i) * KFC + u]
                block = block_ref[k // 2, k % 2]
                kept = []
                for t in range(NY):
                    g = lax.rem(y + t, NY)
                    on = keep_ref[((x * n_i + i) * KFC + u) * NY + g] > 0
                    tile = block[:, t * B : (t + 1) * B]
                    kept.append(jnp.where(on, tile, jnp.zeros_like(tile)))
                right.append(jnp.concatenate(kept, axis=1))
            total += jnp.dot(
                jnp.concatenate(left, axis=1), jnp.concatenate(right, axis=0), preferred_element_type=jnp.float32
            )

        @pl.when(x == 0)
        def _():
            total_ref[i] = total

        @pl.when(x > 0)
        def _():
            total_ref[i] += total

        return carry

    lax.fori_loop(0, n_i, multiply, 0)

    @pl.when(x == NX - 1)
    def _():
        for t in range(NY):
            for i in range(n_i):
                out_refs[t][i] = total_ref[i, :, t * B : (t + 1) * B]


def per_device(factor, index, keep, panel):
    n_i = factor.shape[0]
    factor, index, keep = factor[:, 0], index[:, 0], keep[:, 0]
    y = lax.axis_index("y")

    factors = lax.all_gather(factor, "x", axis=0)

    shard = panel.reshape(NBC, NX, PER_X // CHUNK, SUB, B).transpose(1, 2, 0, 3, 4).reshape(NX, PER_X, B)
    small = jnp.concatenate(
        [
            jnp.broadcast_to(index[None], (NX, n_i, KFC)),
            keep.reshape(n_i, KFC, NX, NY).transpose(2, 0, 1, 3).reshape(NX, n_i, KFC * NY),
        ],
        axis=2,
    ).astype(jnp.bfloat16)
    small = jnp.pad(small, ((0, 0), (0, EXTRA - n_i), (0, B - KFC - KFC * NY)))
    mine = lax.all_to_all(jnp.concatenate([shard, small], axis=1), "x", 0, 0, tiled=True)
    small = mine[:, PER_X : PER_X + n_i].astype(jnp.int32)
    indices = small[:, :, :KFC].reshape(-1)
    keeps = small[:, :, KFC : KFC + KFC * NY].reshape(-1)

    code = pl.pallas_call(
        code_kernel,
        out_shape=jax.ShapeDtypeStruct((SHARD + EXTRA, B), jnp.int16),
        compiler_params=pltpu.CompilerParams(vmem_limit_bytes=32 * MIB),
    )(mine)
    gathered = lax.all_gather(code, ("z", "core"), axis=0)

    smem = pl.BlockSpec(memory_space=pltpu.SMEM)
    tile = jax.ShapeDtypeStruct((n_i, B, B), jnp.float32)
    parts = pl.pallas_call(
        product_kernel,
        grid=(NX,),
        in_specs=[
            smem,
            smem,
            smem,
            pl.BlockSpec((1, n_i, KFC, B, B), lambda x: (x, 0, 0, 0, 0)),
            pl.BlockSpec(memory_space=pltpu.VMEM),
        ],
        out_specs=[pl.BlockSpec((n_i, B, B), lambda x: (0, 0, 0))] * NY,
        out_shape=[tile] * NY,
        scratch_shapes=[
            pltpu.VMEM((NBC // 2, 2, B, NY * B), jnp.bfloat16),
            pltpu.VMEM((n_i, B, NY * B), jnp.float32),
            pltpu.VMEM((ROWS, 8, B), jnp.float32),
        ],
        compiler_params=pltpu.CompilerParams(vmem_limit_bytes=28 * MIB),
        cost_estimate=pl.CostEstimate(flops=2 * 2**30, bytes_accessed=13 * MIB, transcendentals=0),
    )(y.reshape(1), indices, keeps, factors, gathered)

    total = parts[0]
    for t in range(1, NY):
        total += lax.ppermute(parts[t], "y", [(i, (i + t) % NY) for i in range(NY)])
    return total.astype(jnp.bfloat16)[:, None]


def solution(mesh):
    fine = Mesh(mesh.devices.reshape(ROWS // 2, 2, NX, NY), ("z", "core", "x", "y"))
    row, col = ("z", "core"), ("x", "y")
    return jax.shard_map(
        per_device,
        mesh=fine,
        in_specs=(
            P(row, col, None, None, None),
            P(row, col, None),
            P(row, col, None, None),
            P(col, None, row, None),
        ),
        out_specs=P(row, col, None, None),
        check_vma=False,
    )
```

```python
import functools

import jax
import jax.numpy as jnp
from jax import lax
from jax.experimental import pallas as pl
from jax.experimental.pallas import tpu as pltpu
from jax.sharding import Mesh, PartitionSpec as P

ROWS = 32
NX = 4
NY = 4
NBC = 16
KFC = 8
SUB = 4
B = 128
CHUNK = NBC * SUB
PER_X = NY * CHUNK
SHARD = NX * PER_X
EXTRA = 16
MIB = 2**20


def code_kernel(shard_ref, code_ref):
    top = jnp.float32(0.0)
    for x in range(NX):
        top = jnp.maximum(top, jnp.max(jnp.abs(shard_ref[x, :PER_X].astype(jnp.float32))))
    lane = lax.broadcasted_iota(jnp.int32, (8, 128), 1)
    power = jnp.int32(126)
    scale = jnp.float32(2.0**126)
    for e in range(-96, 3):
        above = top >= jnp.float32(2.0**e)
        power = jnp.where(above, jnp.int32(29 - e), power)
        scale = jnp.where(above, jnp.float32(2.0 ** (29 - e)), scale)
    for x in range(NX):

        def step(t, carry):
            rows = pl.ds(pl.multiple_of(t * 16, 16), 16)
            value = shard_ref[x, rows].astype(jnp.float32) * scale
            size = jnp.abs(value)
            high = jnp.full(value.shape, 23 * 512, jnp.int32)
            down = jnp.ones(value.shape, jnp.float32)
            for s in range(1, 23):
                above = size >= jnp.float32(2.0 ** (7 + s))
                high = jnp.where(above, jnp.int32((23 - s) * 512), high)
                down = jnp.where(above, jnp.float32(2.0**-s), down)
            mantissa = jnp.round(value * down).astype(jnp.int32) & 511
            code_ref[pl.ds(pl.multiple_of(x * PER_X + t * 16, 16), 16)] = (high + mantissa).astype(jnp.int16)
            return carry

        lax.fori_loop(0, PER_X // 16, step, 0)
    code_ref[SHARD:] = jnp.full((EXTRA, B), power, jnp.int32).astype(jnp.int16)


def product_kernel(turns, place_ref, index_ref, keep_ref, *refs):
    n_t = len(turns)
    factor_refs, panel_ref, out_refs = refs[:NX], refs[NX], refs[NX + 1 : NX + 1 + n_t]
    code_ref, power_ref, scale_ref, block_a, block_b, sems, power_sem = refs[NX + 1 + n_t :]
    x, y = place_ref[0], place_ref[1]
    n_i = out_refs[0].shape[0]
    home = [lax.rem(x + NX - s, NX) for s in range(NX)]
    turn = [lax.rem(y + t, NY) for t in turns]

    copies = []
    for s in range(NX):
        for t in range(n_t):
            rows = pl.ds(pl.multiple_of(home[s] * PER_X + turn[t] * CHUNK, CHUNK), CHUNK)
            copies.append(pltpu.make_async_copy(panel_ref.at[:, rows], code_ref.at[s, t], sems.at[s, t]))
    powers = pltpu.make_async_copy(panel_ref.at[:, pl.ds(SHARD, EXTRA)], power_ref, power_sem)
    powers.start()
    for copy in copies:
        copy.start()
    for t in range(n_t):
        out_refs[t][...] = jnp.zeros_like(out_refs[t])
    powers.wait()
    power = power_ref[...].astype(jnp.int32)
    scale = jnp.ones(power.shape, jnp.float32)
    for bit in range(7):
        on = (power & (1 << bit)) > 0
        scale = scale * jnp.where(on, jnp.float32(2.0 ** -(1 << bit)), jnp.float32(1.0))
    scale_ref[...] = scale[:, :8]
    low = lax.broadcasted_iota(jnp.int32, (NBC // 2, 8, B), 1) < SUB

    def spread(s, q, block_ref):
        for t in range(n_t):
            piece = []
            for r in range(4):
                code = code_ref[s, t, q * 4 + r].astype(jnp.int32)
                value = lax.shift_right_arithmetic(lax.shift_left(code, 23), lax.shift_right_logical(code, 9))
                piece.append(value.astype(jnp.float32).reshape(NBC // 2, 8, B) * scale_ref[q * 4 + r])
            even, odd = [], []
            for a, b in ((piece[0], piece[1]), (piece[2], piece[3])):
                even.append(jnp.where(low, a, pltpu.roll(b, SUB, 1)))
                odd.append(jnp.where(low, pltpu.roll(a, SUB, 1), b))
            at = pl.ds(pl.multiple_of(q * 16, 16), 16)
            lanes = slice(t * B, (t + 1) * B)
            block_ref[:, 0, at, lanes] = jnp.concatenate(even, axis=1).astype(jnp.bfloat16)
            block_ref[:, 1, at, lanes] = jnp.concatenate(odd, axis=1).astype(jnp.bfloat16)

    def multiply(s, i, block_ref):
        total = jnp.zeros((B, n_t * B), jnp.float32)
        for u in range(0, KFC, 2):
            left, right = [], []
            for v in (u, u + 1):
                entry = (home[s] * n_i + i) * KFC + v
                left.append(factor_refs[s][i, v])
                k = index_ref[entry]
                block = block_ref[k // 2, k % 2]
                kept = []
                for t in range(n_t):
                    tile = block[:, t * B : (t + 1) * B]
                    kept.append(jnp.where(keep_ref[entry * NY + turn[t]] > 0, tile, jnp.zeros_like(tile)))
                right.append(jnp.concatenate(kept, axis=1))
            total += jnp.dot(
                jnp.concatenate(left, axis=1), jnp.concatenate(right, axis=0), preferred_element_type=jnp.float32
            )
        for t in range(n_t):
            out_refs[t][i] += total[:, t * B : (t + 1) * B]

    def arrive(s):
        for copy in copies[s * n_t : (s + 1) * n_t]:
            copy.wait()

    blocks = (block_a, block_b)
    arrive(0)

    def first(q, carry):
        spread(0, q, block_a)
        return carry

    lax.fori_loop(0, ROWS // 4, first, 0)
    for s in range(NX):
        if s + 1 < NX:
            arrive(s + 1)

        def step(i, carry, s=s):
            multiply(s, i, blocks[s % 2])
            if s + 1 < NX:
                for h in range(ROWS // 4 // n_i):
                    spread(s + 1, i * (ROWS // 4 // n_i) + h, blocks[(s + 1) % 2])
            return carry

        lax.fori_loop(0, n_i, step, 0)


def products(turns, place, indices, keeps, factors, gathered):
    n_i, n_t = factors[0].shape[0], len(turns)
    smem = pl.BlockSpec(memory_space=pltpu.SMEM)
    vmem = pl.BlockSpec(memory_space=pltpu.VMEM)
    return pl.pallas_call(
        functools.partial(product_kernel, turns),
        in_specs=[smem] * 3 + [vmem] * NX + [pl.BlockSpec(memory_space=pltpu.HBM)],
        out_specs=[vmem] * n_t,
        out_shape=[jax.ShapeDtypeStruct((n_i, B, B), jnp.float32)] * n_t,
        scratch_shapes=[
            pltpu.VMEM((NX, n_t, ROWS, CHUNK, B), jnp.int16),
            pltpu.VMEM((ROWS, EXTRA, B), jnp.int16),
            pltpu.VMEM((ROWS, 8, B), jnp.float32),
            pltpu.VMEM((NBC // 2, 2, B, n_t * B), jnp.bfloat16),
            pltpu.VMEM((NBC // 2, 2, B, n_t * B), jnp.bfloat16),
            pltpu.SemaphoreType.DMA((NX, n_t)),
            pltpu.SemaphoreType.DMA,
        ],
        compiler_params=pltpu.CompilerParams(vmem_limit_bytes=24 * MIB),
        cost_estimate=pl.CostEstimate(flops=n_t * 2**29, bytes_accessed=n_t * 3 * MIB, transcendentals=0),
    )(place, indices, keeps, *factors, gathered)


def per_device(factor, index, keep, panel):
    n_i = factor.shape[0]
    factor, index, keep = factor[:, 0], index[:, 0], keep[:, 0]
    place = jnp.stack([lax.axis_index("x"), lax.axis_index("y")]).astype(jnp.int32)

    factors = [factor]
    for s in range(1, NX):
        factors.append(lax.ppermute(factor, "x", [(i, (i + s) % NX) for i in range(NX)]))

    shard = panel.reshape(NBC, NX, PER_X // CHUNK, SUB, B).transpose(1, 2, 0, 3, 4).reshape(NX, PER_X, B)
    small = jnp.concatenate(
        [
            jnp.broadcast_to(index[None], (NX, n_i, KFC)),
            keep.reshape(n_i, KFC, NX, NY).transpose(2, 0, 1, 3).reshape(NX, n_i, KFC * NY),
        ],
        axis=2,
    ).astype(jnp.bfloat16)
    small = jnp.pad(small, ((0, 0), (0, EXTRA - n_i), (0, B - KFC - KFC * NY)))
    mine = lax.all_to_all(jnp.concatenate([shard, small], axis=1), "x", 0, 0, tiled=True)
    small = mine[:, PER_X : PER_X + n_i].astype(jnp.int32)
    indices = small[:, :, :KFC].reshape(-1)
    keeps = small[:, :, KFC : KFC + KFC * NY].reshape(-1)

    code = pl.pallas_call(
        code_kernel,
        out_shape=jax.ShapeDtypeStruct((SHARD + EXTRA, B), jnp.int16),
        compiler_params=pltpu.CompilerParams(vmem_limit_bytes=32 * MIB),
    )(mine)
    gathered = lax.all_gather(code, ("z", "core"), axis=0)
    parts = {}
    for turns in ((2,), (1, 3), (0,)):
        for t, part in zip(turns, products(turns, place, indices, keeps, factors, gathered)):
            parts[t] = lax.ppermute(part, "y", [(i, (i + t) % NY) for i in range(NY)]) if t else part
    total = parts[0] + parts[1] + parts[3] + parts[2]
    return total.astype(jnp.bfloat16)[:, None]


def solution(mesh):
    fine = Mesh(mesh.devices.reshape(ROWS // 2, 2, NX, NY), ("z", "core", "x", "y"))
    row, col = ("z", "core"), ("x", "y")
    return jax.shard_map(
        per_device,
        mesh=fine,
        in_specs=(
            P(row, col, None, None, None),
            P(row, col, None),
            P(row, col, None, None),
            P(col, None, row, None),
        ),
        out_specs=P(row, col, None, None),
        check_vma=False,
    )
```

```python
import functools

import jax
import jax.numpy as jnp
from jax import lax
from jax.experimental import pallas as pl
from jax.experimental.pallas import tpu as pltpu
from jax.sharding import Mesh, PartitionSpec as P

ROWS = 32
NX = 4
NY = 4
NBC = 16
KFC = 8
SUB = 4
B = 128
CHUNK = NBC * SUB
PER_X = NY * CHUNK
SHARD = NX * PER_X
EXTRA = 16
MIB = 2**20


def code_kernel(shard_ref, code_ref):
    top = jnp.float32(0.0)
    for x in range(NX):
        top = jnp.maximum(top, jnp.max(jnp.abs(shard_ref[x, :PER_X].astype(jnp.float32))))
    lane = lax.broadcasted_iota(jnp.int32, (8, 128), 1)
    power = jnp.int32(126)
    scale = jnp.float32(2.0**126)
    for e in range(-96, 3):
        above = top >= jnp.float32(2.0**e)
        power = jnp.where(above, jnp.int32(29 - e), power)
        scale = jnp.where(above, jnp.float32(2.0 ** (29 - e)), scale)
    for x in range(NX):

        def step(t, carry):
            rows = pl.ds(pl.multiple_of(t * 16, 16), 16)
            value = shard_ref[x, rows].astype(jnp.float32) * scale
            size = jnp.abs(value)
            high = jnp.full(value.shape, 23 * 512, jnp.int32)
            down = jnp.ones(value.shape, jnp.float32)
            for s in range(1, 23):
                above = size >= jnp.float32(2.0 ** (7 + s))
                high = jnp.where(above, jnp.int32((23 - s) * 512), high)
                down = jnp.where(above, jnp.float32(2.0**-s), down)
            mantissa = jnp.round(value * down).astype(jnp.int32) & 511
            code_ref[pl.ds(pl.multiple_of(x * PER_X + t * 16, 16), 16)] = (high + mantissa).astype(jnp.int16)
            return carry

        lax.fori_loop(0, PER_X // 16, step, 0)
    code_ref[SHARD:] = jnp.full((EXTRA, B), power, jnp.int32).astype(jnp.int16)


def product_kernel(turns, place_ref, index_ref, keep_ref, factors_ref, panel_ref, out_ref, *refs):
    n_t, n_i = len(turns), factors_ref.shape[1]
    code_ref, factor_ref, power_ref, scale_ref, block_a, block_b, sems, factor_sems, power_sem = refs
    y = place_ref[0]
    turn = [lax.rem(y + t, NY) for t in turns]
    slot = turn if out_ref.shape[0] == NY else [0]

    copies = []
    for x in range(NX):
        for t in range(n_t):
            rows = pl.ds(pl.multiple_of(x * PER_X + turn[t] * CHUNK, CHUNK), CHUNK)
            copies.append(pltpu.make_async_copy(panel_ref.at[:, rows], code_ref.at[x, t], sems.at[x, t]))
        copies.append(pltpu.make_async_copy(factors_ref.at[x], factor_ref.at[x], factor_sems.at[x]))
    powers = pltpu.make_async_copy(panel_ref.at[:, pl.ds(SHARD, EXTRA)], power_ref, power_sem)
    powers.start()
    for copy in copies:
        copy.start()
    out_ref[...] = jnp.zeros_like(out_ref)
    powers.wait()
    power = power_ref[...].astype(jnp.int32)
    scale = jnp.ones(power.shape, jnp.float32)
    for bit in range(7):
        on = (power & (1 << bit)) > 0
        scale = scale * jnp.where(on, jnp.float32(2.0 ** -(1 << bit)), jnp.float32(1.0))
    scale_ref[...] = scale[:, :8]
    low = lax.broadcasted_iota(jnp.int32, (NBC // 2, 8, B), 1) < SUB

    def spread(x, q, block_ref):
        for t in range(n_t):
            piece = []
            for r in range(4):
                code = code_ref[x, t, q * 4 + r].astype(jnp.int32)
                value = lax.shift_right_arithmetic(lax.shift_left(code, 23), lax.shift_right_logical(code, 9))
                piece.append(value.astype(jnp.float32).reshape(NBC // 2, 8, B) * scale_ref[q * 4 + r])
            even, odd = [], []
            for a, b in ((piece[0], piece[1]), (piece[2], piece[3])):
                even.append(jnp.where(low, a, pltpu.roll(b, SUB, 1)))
                odd.append(jnp.where(low, pltpu.roll(a, SUB, 1), b))
            at = pl.ds(pl.multiple_of(q * 16, 16), 16)
            lanes = slice(t * B, (t + 1) * B)
            block_ref[:, 0, at, lanes] = jnp.concatenate(even, axis=1).astype(jnp.bfloat16)
            block_ref[:, 1, at, lanes] = jnp.concatenate(odd, axis=1).astype(jnp.bfloat16)

    def multiply(x, i, block_ref):
        total = jnp.zeros((B, n_t * B), jnp.float32)
        for u in range(0, KFC, 2):
            left, right = [], []
            for v in (u, u + 1):
                entry = (x * n_i + i) * KFC + v
                left.append(factor_ref[x, i, v])
                k = index_ref[entry]
                block = block_ref[k // 2, k % 2]
                kept = []
                for t in range(n_t):
                    tile = block[:, t * B : (t + 1) * B]
                    kept.append(jnp.where(keep_ref[entry * NY + turn[t]] > 0, tile, jnp.zeros_like(tile)))
                right.append(jnp.concatenate(kept, axis=1))
            total += jnp.dot(
                jnp.concatenate(left, axis=1), jnp.concatenate(right, axis=0), preferred_element_type=jnp.float32
            )
        for t in range(n_t):
            out_ref[slot[t], i] += total[:, t * B : (t + 1) * B]

    def arrive(x):
        for copy in copies[x * (n_t + 1) : (x + 1) * (n_t + 1)]:
            copy.wait()

    blocks = (block_a, block_b)
    arrive(0)

    def first(q, carry):
        spread(0, q, block_a)
        return carry

    lax.fori_loop(0, ROWS // 4, first, 0)
    per_i = ROWS // 4 // n_i
    for x in range(NX):
        if x + 1 < NX:
            arrive(x + 1)
        for i in range(n_i):
            multiply(x, i, blocks[x % 2])
            if x + 1 < NX:
                for h in range(per_i):
                    spread(x + 1, i * per_i + h, blocks[(x + 1) % 2])


def products(turns, n_out, place, indices, keeps, factors, gathered):
    n_i, n_t = factors.shape[1], len(turns)
    smem = pl.BlockSpec(memory_space=pltpu.SMEM)
    vmem = pl.BlockSpec(memory_space=pltpu.VMEM)
    return pl.pallas_call(
        functools.partial(product_kernel, turns),
        in_specs=[smem] * 3 + [pl.BlockSpec(memory_space=pltpu.HBM)] * 2,
        out_specs=vmem,
        out_shape=jax.ShapeDtypeStruct((n_out, n_i, B, B), jnp.float32),
        scratch_shapes=[
            pltpu.VMEM((NX, n_t, ROWS, CHUNK, B), jnp.int16),
            pltpu.VMEM(factors.shape, jnp.bfloat16),
            pltpu.VMEM((ROWS, EXTRA, B), jnp.int16),
            pltpu.VMEM((ROWS, 8, B), jnp.float32),
            pltpu.VMEM((NBC // 2, 2, B, n_t * B), jnp.bfloat16),
            pltpu.VMEM((NBC // 2, 2, B, n_t * B), jnp.bfloat16),
            pltpu.SemaphoreType.DMA((NX, n_t)),
            pltpu.SemaphoreType.DMA((NX,)),
            pltpu.SemaphoreType.DMA,
        ],
        compiler_params=pltpu.CompilerParams(vmem_limit_bytes=56 * MIB),
        cost_estimate=pl.CostEstimate(flops=n_t * 2**29, bytes_accessed=n_t * 3 * MIB, transcendentals=0),
    )(place, indices, keeps, factors, gathered)


def per_device(factor, index, keep, panel):
    n_i = factor.shape[0]
    factor, index, keep = factor[:, 0], index[:, 0], keep[:, 0]
    place = lax.axis_index("y").astype(jnp.int32).reshape(1)

    factors = lax.all_to_all(jnp.broadcast_to(factor[None], (NX,) + factor.shape), "x", 0, 0, tiled=True)

    shard = panel.reshape(NBC, NX, PER_X // CHUNK, SUB, B).transpose(1, 2, 0, 3, 4).reshape(NX, PER_X, B)
    small = jnp.concatenate(
        [
            jnp.broadcast_to(index[None], (NX, n_i, KFC)),
            keep.reshape(n_i, KFC, NX, NY).transpose(2, 0, 1, 3).reshape(NX, n_i, KFC * NY),
        ],
        axis=2,
    ).astype(jnp.bfloat16)
    small = jnp.pad(small, ((0, 0), (0, EXTRA - n_i), (0, B - KFC - KFC * NY)))
    mine = lax.all_to_all(jnp.concatenate([shard, small], axis=1), "x", 0, 0, tiled=True)
    small = mine[:, PER_X : PER_X + n_i].astype(jnp.int32)
    indices = small[:, :, :KFC].reshape(-1)
    keeps = small[:, :, KFC : KFC + KFC * NY].reshape(-1)

    code = pl.pallas_call(
        code_kernel,
        out_shape=jax.ShapeDtypeStruct((SHARD + EXTRA, B), jnp.int16),
        compiler_params=pltpu.CompilerParams(vmem_limit_bytes=32 * MIB),
    )(mine)
    gathered = lax.all_gather(code, ("z", "core"), axis=0)
    args = (place, indices, keeps, factors, gathered)
    others = lax.all_to_all(products((1, 2, 3), NY, *args), "y", 0, 0, tiled=True)
    total = products((0,), 1, *args)[0] + others[0] + others[1] + others[2] + others[3]
    return total.astype(jnp.bfloat16)[:, None]


def solution(mesh):
    fine = Mesh(mesh.devices.reshape(ROWS // 2, 2, NX, NY), ("z", "core", "x", "y"))
    row, col = ("z", "core"), ("x", "y")
    return jax.shard_map(
        per_device,
        mesh=fine,
        in_specs=(
            P(row, col, None, None, None),
            P(row, col, None),
            P(row, col, None, None),
            P(col, None, row, None),
        ),
        out_specs=P(row, col, None, None),
        check_vma=False,
    )
```

```python
import functools

import jax
import jax.numpy as jnp
from jax import lax
from jax.experimental import pallas as pl
from jax.experimental.pallas import tpu as pltpu
from jax.sharding import Mesh, PartitionSpec as P

ROWS = 32
NX = 4
NY = 4
NBC = 16
KFC = 8
SUB = 4
B = 128
CHUNK = NBC * SUB
PER_X = NY * CHUNK
SHARD = NX * PER_X
EXTRA = 16
MIB = 2**20


def code_kernel(shard_ref, code_ref, small_ref):
    top = jnp.float32(0.0)
    for x in range(NX):
        top = jnp.maximum(top, jnp.max(jnp.abs(shard_ref[x, :PER_X].astype(jnp.float32))))
    lane = lax.broadcasted_iota(jnp.int32, (8, 128), 1)
    power = jnp.int32(126)
    scale = jnp.float32(2.0**126)
    for e in range(-96, 3):
        above = top >= jnp.float32(2.0**e)
        power = jnp.where(above, jnp.int32(29 - e), power)
        scale = jnp.where(above, jnp.float32(2.0 ** (29 - e)), scale)
    for x in range(NX):

        def step(t, carry):
            rows = pl.ds(pl.multiple_of(t * 16, 16), 16)
            value = shard_ref[x, rows].astype(jnp.float32) * scale
            size = jnp.abs(value)
            high = jnp.full(value.shape, 23 * 512, jnp.int32)
            down = jnp.ones(value.shape, jnp.float32)
            for s in range(1, 23):
                above = size >= jnp.float32(2.0 ** (7 + s))
                high = jnp.where(above, jnp.int32((23 - s) * 512), high)
                down = jnp.where(above, jnp.float32(2.0**-s), down)
            mantissa = jnp.round(value * down).astype(jnp.int32) & 511
            code_ref[pl.ds(pl.multiple_of(x * PER_X + t * 16, 16), 16)] = (high + mantissa).astype(jnp.int16)
            return carry

        lax.fori_loop(0, PER_X // 16, step, 0)
    small_ref[...] = shard_ref[:, PER_X:].astype(jnp.int32).reshape(NX * EXTRA, B)
    code_ref[SHARD:] = jnp.full((EXTRA, B), power, jnp.int32).astype(jnp.int16)


def product_kernel(turns, place_ref, small_ref, *refs):
    n_t = len(turns)
    factor_refs, panel_ref, out_refs = refs[:NX], refs[NX], refs[NX + 1 : NX + 1 + n_t]
    code_ref, power_ref, scale_ref, block_a, block_b, sems, power_sem = refs[NX + 1 + n_t :]
    n_i = factor_refs[0].shape[0]
    x, y = place_ref[0], place_ref[1]
    home = [lax.rem(x + NX - s, NX) for s in range(NX)]
    turn = [lax.rem(y + t, NY) for t in turns]

    copies = []
    for s in range(NX):
        for t in range(n_t):
            rows = pl.ds(pl.multiple_of(home[s] * PER_X + turn[t] * CHUNK, CHUNK), CHUNK)
            copies.append(pltpu.make_async_copy(panel_ref.at[:, rows], code_ref.at[s, t], sems.at[s, t]))
    powers = pltpu.make_async_copy(panel_ref.at[:, pl.ds(SHARD, EXTRA)], power_ref, power_sem)
    powers.start()
    for copy in copies:
        copy.start()
    powers.wait()
    power = power_ref[...].astype(jnp.int32)
    scale = jnp.ones(power.shape, jnp.float32)
    for bit in range(7):
        on = (power & (1 << bit)) > 0
        scale = scale * jnp.where(on, jnp.float32(2.0 ** -(1 << bit)), jnp.float32(1.0))
    scale_ref[...] = scale[:, :8]
    low = lax.broadcasted_iota(jnp.int32, (NBC // 2, 8, B), 1) < SUB

    def spread(s, q, t, block_ref):
        piece = []
        for r in range(4):
            code = code_ref[s, t, q * 4 + r].astype(jnp.int32)
            value = lax.shift_right_arithmetic(lax.shift_left(code, 23), lax.shift_right_logical(code, 9))
            piece.append(value.astype(jnp.float32).reshape(NBC // 2, 8, B) * scale_ref[q * 4 + r])
        even, odd = [], []
        for a, b in ((piece[0], piece[1]), (piece[2], piece[3])):
            even.append(jnp.where(low, a, pltpu.roll(b, SUB, 1)))
            odd.append(jnp.where(low, pltpu.roll(a, SUB, 1), b))
        at = pl.ds(pl.multiple_of(q * 16, 16), 16)
        lanes = slice(t * B, (t + 1) * B)
        block_ref[:, 0, at, lanes] = jnp.concatenate(even, axis=1).astype(jnp.bfloat16)
        block_ref[:, 1, at, lanes] = jnp.concatenate(odd, axis=1).astype(jnp.bfloat16)

    def multiply(s, i, u, block_ref):
        left, right = [], []
        for v in (u, u + 1):
            row = home[s] * EXTRA + i
            left.append(factor_refs[s][i, v])
            k = small_ref[row, v]
            block = block_ref[k // 2, k % 2]
            kept = []
            for t in range(n_t):
                tile = block[:, t * B : (t + 1) * B]
                kept.append(jnp.where(small_ref[row, KFC + v * NY + turn[t]] > 0, tile, jnp.zeros_like(tile)))
            right.append(jnp.concatenate(kept, axis=1))
        return jnp.dot(
            jnp.concatenate(left, axis=1), jnp.concatenate(right, axis=0), preferred_element_type=jnp.float32
        )

    def arrive(s):
        for copy in copies[s * n_t : (s + 1) * n_t]:
            copy.wait()

    blocks = (block_a, block_b)
    arrive(0)

    def first(q, carry):
        for t in range(n_t):
            spread(0, q, t, block_a)
        return carry

    lax.fori_loop(0, ROWS // 4, first, 0)
    for s in range(NX):
        pieces = [(q, t) for q in range(ROWS // 4) for t in range(n_t)] if s + 1 < NX else []
        if s + 1 < NX:
            arrive(s + 1)
        for i in range(n_i):
            total = None
            for u in range(0, KFC, 2):
                part = multiply(s, i, u, blocks[s % 2])
                total = part if total is None else total + part
                n = i * (KFC // 2) + u // 2
                n_dots = n_i * KFC // 2
                for q, t in pieces[len(pieces) * n // n_dots : len(pieces) * (n + 1) // n_dots]:
                    spread(s + 1, q, t, blocks[(s + 1) % 2])
            for t in range(n_t):
                part = total[:, t * B : (t + 1) * B]
                out_refs[t][i] = part if s == 0 else out_refs[t][i] + part


def products(turns, place, small, factors, gathered):
    n_i, n_t = factors[0].shape[0], len(turns)
    smem = pl.BlockSpec(memory_space=pltpu.SMEM)
    vmem = pl.BlockSpec(memory_space=pltpu.VMEM)
    return pl.pallas_call(
        functools.partial(product_kernel, turns),
        in_specs=[smem] * 2 + [vmem] * NX + [pl.BlockSpec(memory_space=pltpu.HBM)],
        out_specs=[vmem] * n_t,
        out_shape=[jax.ShapeDtypeStruct((n_i, B, B), jnp.float32)] * n_t,
        scratch_shapes=[
            pltpu.VMEM((NX, n_t, ROWS, CHUNK, B), jnp.int16),
            pltpu.VMEM((ROWS, EXTRA, B), jnp.int16),
            pltpu.VMEM((ROWS, 8, B), jnp.float32),
            pltpu.VMEM((NBC // 2, 2, B, n_t * B), jnp.bfloat16),
            pltpu.VMEM((NBC // 2, 2, B, n_t * B), jnp.bfloat16),
            pltpu.SemaphoreType.DMA((NX, n_t)),
            pltpu.SemaphoreType.DMA,
        ],
        compiler_params=pltpu.CompilerParams(vmem_limit_bytes=47 * MIB),
        cost_estimate=pl.CostEstimate(flops=n_t * 2**29, bytes_accessed=n_t * 3 * MIB, transcendentals=0),
    )(place, small, *factors, gathered)


def per_device(factor, index, keep, panel):
    n_i = factor.shape[0]
    factor, index, keep = factor[:, 0], index[:, 0], keep[:, 0]
    place = jnp.stack([lax.axis_index("x"), lax.axis_index("y")]).astype(jnp.int32)

    factors = [factor]
    for s in range(1, NX):
        factors.append(lax.ppermute(factor, "x", [(i, (i + s) % NX) for i in range(NX)]))

    shard = panel.reshape(NBC, NX, PER_X // CHUNK, SUB, B).transpose(1, 2, 0, 3, 4).reshape(NX, PER_X, B)
    small = jnp.concatenate(
        [
            jnp.broadcast_to(index[None], (NX, n_i, KFC)),
            keep.reshape(n_i, KFC, NX, NY).transpose(2, 0, 1, 3).reshape(NX, n_i, KFC * NY),
        ],
        axis=2,
    ).astype(jnp.bfloat16)
    small = jnp.pad(small, ((0, 0), (0, EXTRA - n_i), (0, B - KFC - KFC * NY)))
    mine = lax.all_to_all(jnp.concatenate([shard, small], axis=1), "x", 0, 0, tiled=True)

    code, small = pl.pallas_call(
        code_kernel,
        out_shape=[
            jax.ShapeDtypeStruct((SHARD + EXTRA, B), jnp.int16),
            jax.ShapeDtypeStruct((NX * EXTRA, B), jnp.int32),
        ],
        compiler_params=pltpu.CompilerParams(vmem_limit_bytes=32 * MIB),
    )(mine)
    gathered = lax.all_gather(code, ("z", "core"), axis=0)
    args = (place, small, factors, gathered)
    away = []
    for t, part in zip((2, 1, 3), products((2, 1, 3), *args)):
        away.append(lax.ppermute(part, "y", [(i, (i + t) % NY) for i in range(NY)]))
    total = products((0,), *args)[0] + away[0] + away[1] + away[2]
    return total.astype(jnp.bfloat16)[:, None]


def solution(mesh):
    fine = Mesh(mesh.devices.reshape(ROWS // 2, 2, NX, NY), ("z", "core", "x", "y"))
    row, col = ("z", "core"), ("x", "y")
    return jax.shard_map(
        per_device,
        mesh=fine,
        in_specs=(
            P(row, col, None, None, None),
            P(row, col, None),
            P(row, col, None, None),
            P(col, None, row, None),
        ),
        out_specs=P(row, col, None, None),
        check_vma=False,
    )
```

```python
import functools

import jax
import jax.numpy as jnp
from jax import lax
from jax.experimental import pallas as pl
from jax.experimental.pallas import tpu as pltpu
from jax.sharding import Mesh, PartitionSpec as P

ROWS = 32
NX = 4
NY = 4
NBC = 16
KFC = 8
SUB = 4
B = 128
CHUNK = NBC * SUB
PER_X = NY * CHUNK
SHARD = NX * PER_X
EXTRA = 16
META = 32
MIB = 2**20


def pack_kernel(panel_hbm, index_hbm, keep_hbm, out_ref, panel_ref, index_ref, keep_ref, sems):
    pairs = ((panel_hbm, panel_ref), (index_hbm, index_ref), (keep_hbm, keep_ref))
    copies = [pltpu.make_async_copy(a, b, sems.at[n]) for n, (a, b) in enumerate(pairs)]
    for copy in copies:
        copy.start()
    for copy in copies:
        copy.wait()
    for g in range(NX * NY):
        rows = panel_ref[:, g].astype(jnp.float32).reshape(CHUNK, B)
        out_ref[g // NY, (g % NY) * CHUNK : (g % NY + 1) * CHUNK] = rows.astype(jnp.bfloat16)
    index = jnp.concatenate(
        [jnp.broadcast_to(index_ref[i : i + 1], (KFC, KFC)) for i in range(META // KFC)], axis=0
    )
    own = lax.broadcasted_iota(jnp.int32, (META, KFC), 0) % KFC == lax.broadcasted_iota(jnp.int32, (META, KFC), 1)
    index = jnp.sum(jnp.where(own, index.astype(jnp.float32), 0.0), axis=1, keepdims=True)
    for x in range(NX):
        out_ref[x, PER_X:] = jnp.zeros((META, B), jnp.bfloat16)
        out_ref[x, PER_X:, : NX * NY] = keep_ref[...].astype(jnp.float32).astype(jnp.bfloat16)
        out_ref[x, PER_X:, NX * NY : NX * NY + 1] = index.astype(jnp.bfloat16)


def code_kernel(shard_ref, code_ref, small_ref):
    top = jnp.float32(0.0)
    for x in range(NX):
        top = jnp.maximum(top, jnp.max(jnp.abs(shard_ref[x, :PER_X].astype(jnp.float32))))
    lane = lax.broadcasted_iota(jnp.int32, (8, 128), 1)
    power = jnp.int32(126)
    scale = jnp.float32(2.0**126)
    for e in range(-96, 3):
        above = top >= jnp.float32(2.0**e)
        power = jnp.where(above, jnp.int32(29 - e), power)
        scale = jnp.where(above, jnp.float32(2.0 ** (29 - e)), scale)
    for x in range(NX):

        def step(t, carry):
            rows = pl.ds(pl.multiple_of(t * 16, 16), 16)
            value = shard_ref[x, rows].astype(jnp.float32) * scale
            high = jnp.full(value.shape, 23 * 512, jnp.int32)
            for s in (16, 8, 4, 2, 1):
                above = jnp.abs(value) >= jnp.float32(2.0 ** (7 + s))
                high = jnp.where(above, high - s * 512, high)
                value = jnp.where(above, value * jnp.float32(2.0**-s), value)
            mantissa = jnp.round(value).astype(jnp.int32) & 511
            code_ref[pl.ds(pl.multiple_of(x * PER_X + t * 16, 16), 16)] = (high + mantissa).astype(jnp.int16)
            return carry

        lax.fori_loop(0, PER_X // 16, step, 0)
    small_ref[...] = shard_ref[:, PER_X:].astype(jnp.int32).reshape(NX * META, B)
    code_ref[SHARD:] = jnp.full((EXTRA, B), power, jnp.int32).astype(jnp.int16)


def product_kernel(turns, place_ref, small_ref, *refs):
    n_t = len(turns)
    factor_refs, panel_ref, out_refs = refs[:NX], refs[NX], refs[NX + 1 : NX + 1 + n_t]
    code_ref, power_ref, scale_ref, block_a, block_b, sems, power_sem = refs[NX + 1 + n_t :]
    n_i = factor_refs[0].shape[0]
    x, y = place_ref[0], place_ref[1]
    home = [lax.rem(x + NX - s, NX) for s in range(NX)]
    turn = [lax.rem(y + t, NY) for t in turns]

    copies = []
    for s in range(NX):
        for t in range(n_t):
            rows = pl.ds(pl.multiple_of(home[s] * PER_X + turn[t] * CHUNK, CHUNK), CHUNK)
            copies.append(pltpu.make_async_copy(panel_ref.at[:, rows], code_ref.at[s, t], sems.at[s, t]))
    powers = pltpu.make_async_copy(panel_ref.at[:, pl.ds(SHARD, EXTRA)], power_ref, power_sem)
    powers.start()
    for copy in copies:
        copy.start()
    powers.wait()
    power = power_ref[...].astype(jnp.int32)
    scale = jnp.ones(power.shape, jnp.float32)
    for bit in range(7):
        on = (power & (1 << bit)) > 0
        scale = scale * jnp.where(on, jnp.float32(2.0 ** -(1 << bit)), jnp.float32(1.0))
    scale_ref[...] = scale[:, :8]
    low = lax.broadcasted_iota(jnp.int32, (NBC // 2, 8, B), 1) < SUB

    def spread(s, q, t, block_ref):
        piece = []
        for r in range(4):
            code = code_ref[s, t, q * 4 + r].astype(jnp.int32)
            value = lax.shift_right_arithmetic(lax.shift_left(code, 23), lax.shift_right_logical(code, 9))
            piece.append(value.astype(jnp.float32).reshape(NBC // 2, 8, B) * scale_ref[q * 4 + r])
        even, odd = [], []
        for a, b in ((piece[0], piece[1]), (piece[2], piece[3])):
            even.append(jnp.where(low, a, pltpu.roll(b, SUB, 1)))
            odd.append(jnp.where(low, pltpu.roll(a, SUB, 1), b))
        at = pl.ds(pl.multiple_of(q * 16, 16), 16)
        lanes = slice(t * B, (t + 1) * B)
        block_ref[:, 0, at, lanes] = jnp.concatenate(even, axis=1).astype(jnp.bfloat16)
        block_ref[:, 1, at, lanes] = jnp.concatenate(odd, axis=1).astype(jnp.bfloat16)

    def multiply(s, i, u, block_ref):
        left, right = [], []
        for v in (u, u + 1):
            row = home[s] * META + i * KFC + v
            left.append(factor_refs[s][i, v])
            k = small_ref[row, NX * NY]
            block = block_ref[k // 2, k % 2]
            kept = []
            for t in range(n_t):
                tile = block[:, t * B : (t + 1) * B]
                kept.append(jnp.where(small_ref[row, x * NY + turn[t]] > 0, tile, jnp.zeros_like(tile)))
            right.append(jnp.concatenate(kept, axis=1))
        return jnp.dot(
            jnp.concatenate(left, axis=1), jnp.concatenate(right, axis=0), preferred_element_type=jnp.float32
        )

    def arrive(s):
        for copy in copies[s * n_t : (s + 1) * n_t]:
            copy.wait()

    blocks = (block_a, block_b)
    arrive(0)

    def first(q, carry):
        for t in range(n_t):
            spread(0, q, t, block_a)
        return carry

    lax.fori_loop(0, ROWS // 4, first, 0)
    for s in range(NX):
        pieces = [(q, t) for q in range(ROWS // 4) for t in range(n_t)] if s + 1 < NX else []
        if s + 1 < NX:
            arrive(s + 1)
        for i in range(n_i):
            total = None
            for u in range(0, KFC, 2):
                part = multiply(s, i, u, blocks[s % 2])
                total = part if total is None else total + part
                n = i * (KFC // 2) + u // 2
                n_dots = n_i * KFC // 2
                for q, t in pieces[len(pieces) * n // n_dots : len(pieces) * (n + 1) // n_dots]:
                    spread(s + 1, q, t, blocks[(s + 1) % 2])
            for t in range(n_t):
                part = total[:, t * B : (t + 1) * B]
                out_refs[t][i] = part if s == 0 else out_refs[t][i] + part


def products(turns, place, small, factors, gathered):
    n_i, n_t = factors[0].shape[0], len(turns)
    smem = pl.BlockSpec(memory_space=pltpu.SMEM)
    vmem = pl.BlockSpec(memory_space=pltpu.VMEM)
    return pl.pallas_call(
        functools.partial(product_kernel, turns),
        in_specs=[smem] * 2 + [vmem] * NX + [pl.BlockSpec(memory_space=pltpu.HBM)],
        out_specs=[vmem] * n_t,
        out_shape=[jax.ShapeDtypeStruct((n_i, B, B), jnp.float32)] * n_t,
        scratch_shapes=[
            pltpu.VMEM((NX, n_t, ROWS, CHUNK, B), jnp.int16),
            pltpu.VMEM((ROWS, EXTRA, B), jnp.int16),
            pltpu.VMEM((ROWS, 8, B), jnp.float32),
            pltpu.VMEM((NBC // 2, 2, B, n_t * B), jnp.bfloat16),
            pltpu.VMEM((NBC // 2, 2, B, n_t * B), jnp.bfloat16),
            pltpu.SemaphoreType.DMA((NX, n_t)),
            pltpu.SemaphoreType.DMA,
        ],
        compiler_params=pltpu.CompilerParams(vmem_limit_bytes=47 * MIB),
        cost_estimate=pl.CostEstimate(flops=n_t * 2**29, bytes_accessed=n_t * 3 * MIB, transcendentals=0),
    )(place, small, *factors, gathered)


def per_device(factor, index, keep, panel):
    n_i = factor.shape[0]
    factor, index, keep = factor[:, 0], index[:, 0], keep[:, 0]
    place = jnp.stack([lax.axis_index("x"), lax.axis_index("y")]).astype(jnp.int32)

    factors = [factor]
    for s in range(1, NX):
        factors.append(lax.ppermute(factor, "x", [(i, (i + s) % NX) for i in range(NX)]))

    packed = pl.pallas_call(
        pack_kernel,
        in_specs=[pl.BlockSpec(memory_space=pltpu.HBM)] * 3,
        out_shape=jax.ShapeDtypeStruct((NX, PER_X + META, B), jnp.bfloat16),
        scratch_shapes=[
            pltpu.VMEM(panel.shape, jnp.bfloat16),
            pltpu.VMEM(index.shape, jnp.int32),
            pltpu.VMEM((n_i * KFC, NX * NY), jnp.int32),
            pltpu.SemaphoreType.DMA((3,)),
        ],
        compiler_params=pltpu.CompilerParams(vmem_limit_bytes=63 * MIB),
    )(panel, index, keep.reshape(n_i * KFC, NX * NY))
    mine = lax.all_to_all(packed, "x", 0, 0, tiled=True)

    code, small = pl.pallas_call(
        code_kernel,
        out_shape=[
            jax.ShapeDtypeStruct((SHARD + EXTRA, B), jnp.int16),
            jax.ShapeDtypeStruct((NX * META, B), jnp.int32),
        ],
        compiler_params=pltpu.CompilerParams(vmem_limit_bytes=32 * MIB),
    )(mine)
    gathered = lax.all_gather(code, ("z", "core"), axis=0)
    args = (place, small, factors, gathered)
    away = []
    for t, part in zip((2, 1, 3), products((2, 1, 3), *args)):
        away.append(lax.ppermute(part, "y", [(i, (i + t) % NY) for i in range(NY)]))
    total = products((0,), *args)[0] + away[0] + away[1] + away[2]
    return total.astype(jnp.bfloat16)[:, None]


def solution(mesh):
    fine = Mesh(mesh.devices.reshape(ROWS // 2, 2, NX, NY), ("z", "core", "x", "y"))
    row, col = ("z", "core"), ("x", "y")
    return jax.shard_map(
        per_device,
        mesh=fine,
        in_specs=(
            P(row, col, None, None, None),
            P(row, col, None),
            P(row, col, None, None),
            P(col, None, row, None),
        ),
        out_specs=P(row, col, None, None),
        check_vma=False,
    )
```

```python
import functools

import jax
import jax.numpy as jnp
from jax import lax
from jax.experimental import pallas as pl
from jax.experimental.pallas import tpu as pltpu
from jax.sharding import Mesh, PartitionSpec as P

ROWS = 32
NX = 4
NY = 4
NBC = 16
KFC = 8
SUB = 4
B = 128
CHUNK = NBC * SUB
PER_X = NY * CHUNK
SHARD = NX * PER_X
EXTRA = 16
META = 32
MIB = 2**20


def pack_kernel(panel_hbm, index_hbm, keep_hbm, out_ref, panel_ref, index_ref, keep_ref, sems):
    pairs = ((panel_hbm, panel_ref), (index_hbm, index_ref), (keep_hbm, keep_ref))
    copies = [pltpu.make_async_copy(a, b, sems.at[n]) for n, (a, b) in enumerate(pairs)]
    for copy in copies:
        copy.start()
    for copy in copies:
        copy.wait()
    for g in range(NX * NY):
        rows = panel_ref[:, g].astype(jnp.float32).reshape(CHUNK, B)
        out_ref[g // NY, (g % NY) * CHUNK : (g % NY + 1) * CHUNK] = rows.astype(jnp.bfloat16)
    index = jnp.concatenate(
        [jnp.broadcast_to(index_ref[i : i + 1], (KFC, KFC)) for i in range(META // KFC)], axis=0
    )
    own = lax.broadcasted_iota(jnp.int32, (META, KFC), 0) % KFC == lax.broadcasted_iota(jnp.int32, (META, KFC), 1)
    index = jnp.sum(jnp.where(own, index.astype(jnp.float32), 0.0), axis=1, keepdims=True)
    for x in range(NX):
        out_ref[x, PER_X:] = jnp.zeros((META, B), jnp.bfloat16)
        out_ref[x, PER_X:, : NX * NY] = keep_ref[...].astype(jnp.float32).astype(jnp.bfloat16)
        out_ref[x, PER_X:, NX * NY : NX * NY + 1] = index.astype(jnp.bfloat16)


def code_kernel(shard_ref, code_ref, small_ref):
    top = jnp.float32(0.0)
    for x in range(NX):
        top = jnp.maximum(top, jnp.max(jnp.abs(shard_ref[x, :PER_X].astype(jnp.float32))))
    lane = lax.broadcasted_iota(jnp.int32, (8, 128), 1)
    power = jnp.int32(126)
    scale = jnp.float32(2.0**126)
    for e in range(-96, 3):
        above = top >= jnp.float32(2.0**e)
        power = jnp.where(above, jnp.int32(29 - e), power)
        scale = jnp.where(above, jnp.float32(2.0 ** (29 - e)), scale)
    for x in range(NX):

        def step(t, carry):
            rows = pl.ds(pl.multiple_of(t * 16, 16), 16)
            value = shard_ref[x, rows].astype(jnp.float32) * scale
            high = jnp.full(value.shape, 23 * 512, jnp.int32)
            for s in (16, 8, 4, 2, 1):
                above = jnp.abs(value) >= jnp.float32(2.0 ** (7 + s))
                high = jnp.where(above, high - s * 512, high)
                value = jnp.where(above, value * jnp.float32(2.0**-s), value)
            mantissa = jnp.round(value).astype(jnp.int32) & 511
            code_ref[pl.ds(pl.multiple_of(x * PER_X + t * 16, 16), 16)] = (high + mantissa).astype(jnp.int16)
            return carry

        lax.fori_loop(0, PER_X // 16, step, 0)
    small_ref[...] = shard_ref[:, PER_X:].astype(jnp.int32).reshape(NX * META, B)
    code_ref[SHARD:] = jnp.full((EXTRA, B), power, jnp.int32).astype(jnp.int16)


def product_kernel(turns, place_ref, small_ref, *refs):
    n_t = len(turns)
    factor_refs, panel_ref, out_refs = refs[:NX], refs[NX], refs[NX + 1 : NX + 1 + n_t]
    code_ref, power_ref, scale_ref, block_a, block_b, sems, power_sem = refs[NX + 1 + n_t :]
    n_i = factor_refs[0].shape[0]
    x, y = place_ref[0], place_ref[1]
    home = [lax.rem(x + NX - s, NX) for s in range(NX)]
    turn = [lax.rem(y + t, NY) for t in turns]

    copies = []
    for s in range(NX):
        for t in range(n_t):
            rows = pl.ds(pl.multiple_of(home[s] * PER_X + turn[t] * CHUNK, CHUNK), CHUNK)
            copies.append(pltpu.make_async_copy(panel_ref.at[:, rows], code_ref.at[s, t], sems.at[s, t]))
    powers = pltpu.make_async_copy(panel_ref.at[:, pl.ds(SHARD, EXTRA)], power_ref, power_sem)
    powers.start()
    for copy in copies:
        copy.start()
    powers.wait()
    power = power_ref[...].astype(jnp.int32)
    scale = jnp.ones(power.shape, jnp.float32)
    for bit in range(7):
        on = (power & (1 << bit)) > 0
        scale = scale * jnp.where(on, jnp.float32(2.0 ** -(1 << bit)), jnp.float32(1.0))
    scale_ref[...] = scale[:, :8]
    low = lax.broadcasted_iota(jnp.int32, (NBC // 2, 8, B), 1) < SUB

    def spread(s, q, t, block_ref):
        piece = []
        for r in range(4):
            code = code_ref[s, t, q * 4 + r].astype(jnp.int32)
            value = lax.shift_right_arithmetic(lax.shift_left(code, 23), lax.shift_right_logical(code, 9))
            piece.append(value.astype(jnp.float32).reshape(NBC // 2, 8, B) * scale_ref[q * 4 + r])
        even, odd = [], []
        for a, b in ((piece[0], piece[1]), (piece[2], piece[3])):
            even.append(jnp.where(low, a, pltpu.roll(b, SUB, 1)))
            odd.append(jnp.where(low, pltpu.roll(a, SUB, 1), b))
        at = pl.ds(pl.multiple_of(q * 16, 16), 16)
        lanes = slice(t * B, (t + 1) * B)
        block_ref[:, 0, at, lanes] = jnp.concatenate(even, axis=1).astype(jnp.bfloat16)
        block_ref[:, 1, at, lanes] = jnp.concatenate(odd, axis=1).astype(jnp.bfloat16)

    def multiply(s, i, u, block_ref):
        left, right = [], []
        for v in (u, u + 1):
            row = home[s] * META + i * KFC + v
            left.append(factor_refs[s][i, v])
            k = small_ref[row, NX * NY]
            block = block_ref[k // 2, k % 2]
            kept = []
            for t in range(n_t):
                tile = block[:, t * B : (t + 1) * B]
                kept.append(jnp.where(small_ref[row, x * NY + turn[t]] > 0, tile, jnp.zeros_like(tile)))
            right.append(jnp.concatenate(kept, axis=1))
        return jnp.dot(
            jnp.concatenate(left, axis=1), jnp.concatenate(right, axis=0), preferred_element_type=jnp.float32
        )

    def arrive(s):
        for copy in copies[s * n_t : (s + 1) * n_t]:
            copy.wait()

    blocks = (block_a, block_b)
    arrive(0)

    def first(q, carry):
        for t in range(n_t):
            spread(0, q, t, block_a)
        return carry

    lax.fori_loop(0, ROWS // 4, first, 0)
    for s in range(NX):
        pieces = [(q, t) for q in range(ROWS // 4) for t in range(n_t)] if s + 1 < NX else []
        if s + 1 < NX:
            arrive(s + 1)
        for i in range(n_i):
            total = None
            for u in range(0, KFC, 2):
                part = multiply(s, i, u, blocks[s % 2])
                total = part if total is None else total + part
                n = i * (KFC // 2) + u // 2
                n_dots = n_i * KFC // 2
                for q, t in pieces[len(pieces) * n // n_dots : len(pieces) * (n + 1) // n_dots]:
                    spread(s + 1, q, t, blocks[(s + 1) % 2])
            for t in range(n_t):
                part = total[:, t * B : (t + 1) * B]
                out_refs[t][i] = part if s == 0 else out_refs[t][i] + part


def products(turns, place, small, factors, gathered):
    n_i, n_t = factors[0].shape[0], len(turns)
    smem = pl.BlockSpec(memory_space=pltpu.SMEM)
    vmem = pl.BlockSpec(memory_space=pltpu.VMEM)
    return pl.pallas_call(
        functools.partial(product_kernel, turns),
        in_specs=[smem] * 2 + [vmem] * NX + [pl.BlockSpec(memory_space=pltpu.HBM)],
        out_specs=[vmem] * n_t,
        out_shape=[jax.ShapeDtypeStruct((n_i, B, B), jnp.float32)] * n_t,
        scratch_shapes=[
            pltpu.VMEM((NX, n_t, ROWS, CHUNK, B), jnp.int16),
            pltpu.VMEM((ROWS, EXTRA, B), jnp.int16),
            pltpu.VMEM((ROWS, 8, B), jnp.float32),
            pltpu.VMEM((NBC // 2, 2, B, n_t * B), jnp.bfloat16),
            pltpu.VMEM((NBC // 2, 2, B, n_t * B), jnp.bfloat16),
            pltpu.SemaphoreType.DMA((NX, n_t)),
            pltpu.SemaphoreType.DMA,
        ],
        compiler_params=pltpu.CompilerParams(vmem_limit_bytes=47 * MIB),
        cost_estimate=pl.CostEstimate(flops=n_t * 2**29, bytes_accessed=n_t * 3 * MIB, transcendentals=0),
    )(place, small, *factors, gathered)


def per_device(factor, index, keep, panel):
    n_i = factor.shape[0]
    factor, index, keep = factor[:, 0], index[:, 0], keep[:, 0]
    place = jnp.stack([lax.axis_index("x"), lax.axis_index("y")]).astype(jnp.int32)

    factors = [factor]
    for s in range(1, NX):
        factors.append(lax.ppermute(factor, "x", [(i, (i + s) % NX) for i in range(NX)]))

    packed = pl.pallas_call(
        pack_kernel,
        in_specs=[pl.BlockSpec(memory_space=pltpu.HBM)] * 3,
        out_shape=jax.ShapeDtypeStruct((NX, PER_X + META, B), jnp.bfloat16),
        scratch_shapes=[
            pltpu.VMEM(panel.shape, jnp.bfloat16),
            pltpu.VMEM(index.shape, jnp.int32),
            pltpu.VMEM((n_i * KFC, NX * NY), jnp.int32),
            pltpu.SemaphoreType.DMA((3,)),
        ],
        compiler_params=pltpu.CompilerParams(vmem_limit_bytes=63 * MIB),
    )(panel, index, keep.reshape(n_i * KFC, NX * NY))
    mine = lax.all_to_all(packed, "x", 0, 0, tiled=True)

    code, small = pl.pallas_call(
        code_kernel,
        out_shape=[
            jax.ShapeDtypeStruct((SHARD + EXTRA, B), jnp.int16),
            jax.ShapeDtypeStruct((NX * META, B), jnp.int32),
        ],
        compiler_params=pltpu.CompilerParams(vmem_limit_bytes=32 * MIB),
    )(mine)
    gathered = lax.all_gather(code, ("z", "core"), axis=0)
    args = (place, small, factors, gathered)
    away = []
    for t, part in zip((3, 2, 1), products((3, 2, 1), *args)):
        away.append(lax.ppermute(part, "y", [(i, (i + t) % NY) for i in range(NY)]))
    total = products((0,), *args)[0] + away[0] + away[1] + away[2]
    return total.astype(jnp.bfloat16)[:, None]


def solution(mesh):
    fine = Mesh(mesh.devices.reshape(ROWS // 2, 2, NX, NY), ("z", "core", "x", "y"))
    row, col = ("z", "core"), ("x", "y")
    return jax.shard_map(
        per_device,
        mesh=fine,
        in_specs=(
            P(row, col, None, None, None),
            P(row, col, None),
            P(row, col, None, None),
            P(col, None, row, None),
        ),
        out_specs=P(row, col, None, None),
        check_vma=False,
    )
```
